32 devices in a mesh: dp: 4 (over x, core), mem: 8 (over z, y).
Axes of the slice: x: 2, y: 2, z: 4, core: 2. Of those that a mesh axis runs over, the one named last changes fastest.
Arguments:
- tokens: bfloat16 [4096, 2048], P(('dp', 'mem')), may hold values from -60 to 60
- norm_gain: float32 [2048], replicated, may hold values from 0.1 to 1.9
- query_weight: bfloat16 [2048, 2048], P(None, 'dp'), may hold values from -0.125 to 0.125
- values: bfloat16 [32768, 2048], P(('dp', 'mem')), may hold values from -6 to 6
- blocks: int32 [4096, 2], P(('dp', 'mem')), may hold values from 0 to 511, as said below
- weights: float32 [4096, 2], P(('dp', 'mem')), may hold values from 0.25 to 1
- out_cotangent: bfloat16 [4096, 2048], P(('dp', 'mem')), may hold values from -6 to 6
Outputs:
- layer_out: float32 [4096, 2048], P(('dp', 'mem'))
- grad_tokens: float32 [4096, 2048], P(('dp', 'mem'))
- grad_values: bfloat16 [32768, 2048], P(('dp', 'mem'))
The draws below stay inside these ranges and needn't reach their ends.
Inputs may be any that keep to these rules, and one draw needn't show every extreme that they name: Block b is held by device b // 16, devices counted as the tokens are (dp major, mem minor). The 2 blocks of one token differ. The tokens of one device make at most 16 lookups (repeats counted) into the blocks held by any one device, and in every draw some devices receive exactly 16 lookups from the tokens of every device.
All inputs are finite; a program needn't handle non-finite values.
Results may differ from the reference program's by a relative error of at most 0.012.
Values may be sent and summed in bfloat16 or wider, within the bound.
A program may use at most 128 MiB of HBM per device.

```python
import math
import jax
import jax.numpy as jnp
from jax import lax

D = 2048
BLOCK = 64
TOPK = 2
TOK = 128
BLK_DEV = 16
VALUES = 32768
TOKENS = 4096
N_DP = 4
N_MEM = 8


def draw_tokens(key, part):
    key_rows, key_cols, key_noise = jax.random.split(key, 3)
    row_scale = jnp.exp(jax.random.uniform(key_rows, (TOKENS, 1), jnp.float32) * math.log(10.0))
    noise = jnp.clip(jax.random.normal(key_noise, (TOKENS, D), jnp.float32), -6.0, 6.0)
    col_scale = jnp.exp(jax.random.uniform(key_cols, (1, D), jnp.float32) * math.log(10.0))
    return (noise * row_scale * col_scale * 0.1).astype(jnp.bfloat16)


def draw_blocks(key, part):
    owner_count = N_DP * N_MEM
    pair_count = TOK * TOPK
    capacity = 2 * pair_count // owner_count
    hot_count = owner_count // 8
    cold_count = owner_count - hot_count
    rest_count = pair_count - hot_count * capacity
    base_count = rest_count // cold_count
    extra_count = rest_count % cold_count
    shuffle_order = jax.random.permutation(jax.random.fold_in(key, 11), owner_count)
    order_rank = jnp.argsort(shuffle_order, stable=True).astype(jnp.int32)

    def one_source(source):
        source_key = jax.random.fold_in(jax.random.fold_in(key, 23), source)
        key_extra, key_shuffle, key_local = jax.random.split(source_key, 3)
        lucky_rank = jax.random.permutation(key_extra, cold_count)
        chosen = jnp.take(lucky_rank, jnp.clip(order_rank - hot_count, 0, cold_count - 1)) < extra_count
        per_owner = jnp.where(order_rank < hot_count, capacity, base_count + chosen.astype(jnp.int32))
        bounds = jnp.cumsum(per_owner)
        owners_of = jnp.searchsorted(bounds, jnp.arange(pair_count, dtype=jnp.int32), side='right').astype(jnp.int32)
        owners_of = owners_of[jax.random.permutation(key_shuffle, pair_count)]
        local_block = jax.random.randint(key_local, (TOK, TOPK), 0, BLK_DEV // TOPK) * TOPK + jnp.arange(TOPK, dtype=jnp.int32)[None, :]
        return owners_of.reshape(TOK, TOPK) * BLK_DEV + local_block
    drawn = jax.vmap(one_source)(jnp.arange(owner_count, dtype=jnp.int32))
    return drawn.reshape(owner_count * TOK, TOPK).astype(jnp.int32)


def levels(key, extent, cuts, least, top_value):
    factor_of = 1.0
    for axis_at, blocks in cuts:
        heights = jax.random.uniform(jax.random.fold_in(jax.random.fold_in(key, 6), axis_at), (blocks,), jnp.float32, least / len(cuts), top_value / len(cuts))
        factor_of = factor_of * jnp.repeat(jnp.exp(heights), extent[axis_at] // blocks).reshape((-1,) + (1,) * (len(extent) - 1 - axis_at))
    return factor_of


def centred(own_key, extent, width, most, cuts=(), kind=jnp.bfloat16):
    values = jax.random.normal(own_key, extent, jnp.float32) * width
    if len(cuts) > 0:
        values = levels(own_key, extent, cuts, -0.22, 0.18) * values
    return jnp.clip(values, min=-most, max=most).astype(kind)


def setup_inputs(seed: int = 0) -> dict:
    key_of = jax.random.split(jax.random.key(seed), 8)
    tokens = draw_tokens(jax.random.fold_in(key_of[7], 71), 0)
    norm_gain = jnp.clip(1.0 + 0.18 * jax.random.normal(key_of[1], (D,), jnp.float32), 0.1, 1.9)
    query_weight = centred(key_of[2], (D, D), D ** -0.5, 0.125, ((1, 4),))
    values = centred(key_of[3], (VALUES, D), 1.0, 6.0, ((0, 32),))
    blocks = draw_blocks(jax.random.fold_in(key_of[7], 71), 0)
    weights = jnp.clip(jnp.exp(math.log(1.0) - 1.3862944 * jax.random.uniform(key_of[5], (TOKENS, TOPK), jnp.float32) ** levels(key_of[5], (TOKENS, TOPK), ((0, 32),), -0.2, 0.2)), 0.25, 1.0)
    out_cotangent = centred(key_of[6], (TOKENS, D), 1.0, 6.0, ((0, 32),))
    return {"tokens": tokens, "norm_gain": norm_gain, "query_weight": query_weight, "values": values, "blocks": blocks, "weights": weights, "out_cotangent": out_cotangent}


def reference(tokens, norm_gain, query_weight, values, blocks, weights, out_cotangent):
    score_scale = float(D) ** (-0.5)
    exact_tokens = tokens.astype(jnp.float32)
    rms_rows = lax.rsqrt(lax.optimization_barrier(jnp.mean(exact_tokens * exact_tokens, axis=1, keepdims=True)) + 1e-06)
    unit_rows = exact_tokens * rms_rows
    normed = (unit_rows * norm_gain).astype(jnp.bfloat16)
    queries = jnp.dot(normed, query_weight, preferred_element_type=jnp.float32).astype(jnp.bfloat16)
    offsets = jnp.arange(BLOCK, dtype=jnp.int32)
    group_count = TOKENS // TOK

    def scan_step(grad_rows, group_index):
        start = (group_index * TOK).astype(jnp.int32)
        query_block = lax.dynamic_slice_in_dim(queries, start, TOK, 0)
        token_block = lax.dynamic_slice_in_dim(exact_tokens, start, TOK, 0)
        cot_block = lax.dynamic_slice_in_dim(out_cotangent, start, TOK, 0).astype(jnp.float32)
        block_ids = lax.dynamic_slice_in_dim(blocks, start, TOK, 0).astype(jnp.int32)
        weight_block = lax.dynamic_slice_in_dim(weights, start, TOK, 0)
        row_ids = (block_ids[:, :, None] * BLOCK + offsets[None, None, :]).astype(jnp.int32)
        gathered = jnp.take(values, row_ids.reshape(-1), axis=0).reshape(TOK, TOPK, BLOCK, D).astype(jnp.float32)
        query_exact = query_block.astype(jnp.float32)
        scores = jnp.einsum('cd,ckjd->ckj', query_exact, gathered) * score_scale
        sigmoid_of = jax.nn.sigmoid(scores)
        gate_values = sigmoid_of.astype(jnp.bfloat16)
        block_parts = jnp.einsum('ckj,ckjd->ckd', gate_values.astype(jnp.float32), gathered).astype(jnp.bfloat16)
        mixed = lax.optimization_barrier(jnp.sum(weight_block[:, :, None] * block_parts.astype(jnp.float32), axis=1))
        out_block = token_block + mixed
        scaled_cot = (weight_block[:, :, None] * cot_block[:, None, :]).astype(jnp.bfloat16)
        cot_scores = jnp.einsum('ckd,ckjd->ckj', scaled_cot.astype(jnp.float32), gathered)
        score_grads = (cot_scores * sigmoid_of * (1.0 - sigmoid_of) * score_scale).astype(jnp.bfloat16)
        query_parts = jnp.einsum('ckj,ckjd->ckd', score_grads.astype(jnp.float32), gathered).astype(jnp.bfloat16)
        query_grad = lax.optimization_barrier(jnp.sum(query_parts.astype(jnp.float32), axis=1)).astype(jnp.bfloat16)
        contrib = gate_values.astype(jnp.float32)[:, :, :, None] * scaled_cot.astype(jnp.float32)[:, :, None, :]
        contrib = contrib + score_grads.astype(jnp.float32)[:, :, :, None] * query_exact[:, None, None, :]
        grad_rows = grad_rows.at[row_ids.reshape(-1)].add(contrib.reshape(-1, D))
        return (grad_rows, (out_block, query_grad))
    grad_rows, (out_blocks, query_grads) = lax.scan(scan_step, jnp.zeros((VALUES, D), jnp.float32), jnp.arange(group_count, dtype=jnp.int32))
    layer_out = out_blocks.reshape(TOKENS, D)
    query_grad = query_grads.reshape(TOKENS, D)
    normed_grad = jnp.dot(query_grad, query_weight.T, preferred_element_type=jnp.float32)
    unit_grad = normed_grad * norm_gain
    grad_tokens = out_cotangent.astype(jnp.float32) + rms_rows * (unit_grad - unit_rows * lax.optimization_barrier(jnp.mean(unit_grad * unit_rows, axis=1, keepdims=True)))
    return (layer_out, grad_tokens, grad_rows.astype(jnp.bfloat16))
```

```python
import jax
import jax.numpy as jnp
from jax import lax
from jax.sharding import PartitionSpec as P

BLOCK = 64
AXES = ("dp", "mem")
BF = jnp.bfloat16
F32 = jnp.float32


def dot(left, right, left_dim=1, right_dim=0):
    return lax.dot_general(
        left, right, (((left_dim,), (right_dim,)), ((), ())), preferred_element_type=F32
    )


def exchange(rows, owner_count):
    slots, features = rows.shape
    out = lax.all_to_all(
        rows.reshape(owner_count, slots // owner_count, features),
        AXES,
        split_axis=0,
        concat_axis=0,
        tiled=True,
    )
    return out.reshape(slots, features)


def body(tokens, norm_gain, query_weight, values, blocks, weights, out_cotangent):
    token_count, features = tokens.shape
    top_count = blocks.shape[1]
    value_rows = values.shape[0]
    span_blocks = value_rows // BLOCK
    owner_count = lax.axis_size("dp") * lax.axis_size("mem")
    pair_count = token_count * top_count
    capacity = 2 * pair_count // owner_count
    slot_total = owner_count * capacity
    score_scale = float(features) ** (-0.5)
    me = lax.axis_index(AXES)

    all_blocks = lax.all_gather(blocks, AXES, axis=0, tiled=True)
    weight_full = lax.all_gather(query_weight, "dp", axis=1, tiled=True)

    earlier = (
        jnp.arange(pair_count)[:, None] > jnp.arange(pair_count)[None, :]
    ).astype(BF)

    flat_ids = blocks.reshape(pair_count)
    owner_of = flat_ids // span_blocks
    hits = owner_of[:, None] == jnp.arange(owner_count, dtype=jnp.int32)[None, :]
    ranks = dot(earlier, hits.astype(BF))
    slot_of = jnp.sum(jnp.where(hits, ranks, 0.0), axis=1).astype(jnp.int32)
    target = (owner_of * capacity + slot_of).reshape(token_count, top_count)
    slot_ids = jnp.arange(slot_total, dtype=jnp.int32)
    picks = [(target[:, k][None, :] == slot_ids[:, None]) for k in range(top_count)]
    pick_rows = sum(p.astype(BF) for p in picks)
    slot_weight = sum(
        jnp.sum(jnp.where(p, weights[:, k][None, :], 0.0), axis=1, keepdims=True)
        for k, p in enumerate(picks)
    )

    cot_load = (slot_weight * dot(pick_rows, out_cotangent)).astype(BF)
    cot_rows = exchange(cot_load, owner_count)

    exact_tokens = tokens.astype(F32)
    rms_rows = lax.rsqrt(jnp.mean(exact_tokens * exact_tokens, axis=1, keepdims=True) + 1e-06)
    unit_rows = exact_tokens * rms_rows
    normed = (unit_rows * norm_gain).astype(BF)
    normed_rows = exchange(dot(pick_rows, normed).astype(BF), owner_count)

    their_ids = all_blocks.reshape(owner_count, pair_count)
    mine = their_ids // span_blocks == me
    their_rank = dot(mine.astype(BF), earlier, 1, 1).astype(jnp.int32)
    rank_here = jnp.where(mine, their_rank, -1)
    local_next = (their_ids % span_blocks + 1)[:, None, :]
    at_slot = rank_here[:, None, :] == jnp.arange(capacity, dtype=jnp.int32)[None, :, None]
    block_here = jnp.sum(jnp.where(at_slot, local_next, 0), axis=2) - 1
    row_block = jnp.arange(value_rows, dtype=jnp.int32) // BLOCK
    in_block = block_here.reshape(slot_total)[:, None] == row_block[None, :]

    cot_scores = dot(cot_rows, values, 1, 1)
    query_rows = dot(normed_rows, weight_full).astype(BF)
    scores = dot(query_rows, values, 1, 1) * score_scale
    sigmoid_of = jax.nn.sigmoid(scores)
    gate_values = jnp.where(in_block, sigmoid_of, 0.0).astype(BF)
    parts_back = exchange(dot(gate_values, values).astype(BF), owner_count)
    score_grads = jnp.where(
        in_block, cot_scores * sigmoid_of * (1.0 - sigmoid_of) * score_scale, 0.0
    ).astype(BF)
    grads_back = exchange(dot(score_grads, values).astype(BF), owner_count)
    grad_values = (dot(gate_values, cot_rows, 0, 0) + dot(score_grads, query_rows, 0, 0)).astype(BF)

    mixed = sum(
        weights[:, k][:, None] * dot(p.astype(BF), parts_back, 0, 0) for k, p in enumerate(picks)
    )
    layer_out = exact_tokens + mixed
    query_grad = dot(pick_rows, grads_back, 0, 0).astype(BF)
    unit_grad = dot(query_grad, weight_full, 1, 1) * norm_gain
    grad_tokens = out_cotangent.astype(F32) + rms_rows * (
        unit_grad - unit_rows * jnp.mean(unit_grad * unit_rows, axis=1, keepdims=True)
    )
    return (layer_out, grad_tokens, grad_values)


def solution(mesh):
    rows = P(AXES, None)
    return jax.shard_map(
        body,
        mesh=mesh,
        in_specs=(rows, P(), P(None, "dp"), rows, rows, rows, rows),
        out_specs=(rows, rows, rows),
        check_vma=False,
    )
```

```python
import jax
import jax.numpy as jnp
from jax import lax
from jax.sharding import PartitionSpec as P

BLOCK = 64
LANES = 128
AXES = ("dp", "mem")
BF = jnp.bfloat16
F32 = jnp.float32


def dot(left, right, left_dim=1, right_dim=0):
    return lax.dot_general(
        left, right, (((left_dim,), (right_dim,)), ((), ())), preferred_element_type=F32
    )


def exchange(rows, owner_count):
    slots, features = rows.shape
    out = lax.all_to_all(
        rows.reshape(owner_count, slots // owner_count, features),
        AXES,
        split_axis=0,
        concat_axis=0,
        tiled=True,
    )
    return out.reshape(slots, features)


def body(tokens, norm_gain, query_weight, values, blocks, weights, out_cotangent):
    token_count, features = tokens.shape
    top_count = blocks.shape[1]
    value_rows = values.shape[0]
    span_blocks = value_rows // BLOCK
    owner_count = lax.axis_size("dp") * lax.axis_size("mem")
    pair_count = token_count * top_count
    capacity = 2 * pair_count // owner_count
    slot_total = owner_count * capacity
    score_scale = float(features) ** (-0.5)
    weight_full = lax.all_gather(query_weight, "dp", axis=1, tiled=True)

    earlier = (
        jnp.arange(pair_count)[:, None] > jnp.arange(pair_count)[None, :]
    ).astype(BF)

    flat_ids = blocks.reshape(pair_count)
    owner_of = flat_ids // span_blocks
    hits = owner_of[:, None] == jnp.arange(owner_count, dtype=jnp.int32)[None, :]
    ranks = dot(earlier, hits.astype(BF))
    slot_of = jnp.sum(jnp.where(hits, ranks, 0.0), axis=1).astype(jnp.int32)
    target = (owner_of * capacity + slot_of).reshape(token_count, top_count)
    slot_ids = jnp.arange(slot_total, dtype=jnp.int32)
    picks = [(target[:, k][None, :] == slot_ids[:, None]) for k in range(top_count)]
    pick_rows = sum(p.astype(BF) for p in picks)
    slot_weight = sum(
        jnp.sum(jnp.where(p, weights[:, k][None, :], 0.0), axis=1, keepdims=True)
        for k, p in enumerate(picks)
    )

    local_next = blocks % span_blocks + 1
    slot_block = sum(
        jnp.sum(jnp.where(p, local_next[:, k][None, :], 0), axis=1, keepdims=True)
        for k, p in enumerate(picks)
    )

    exact_tokens = tokens.astype(F32)
    rms_rows = lax.rsqrt(jnp.mean(exact_tokens * exact_tokens, axis=1, keepdims=True) + 1e-06)
    unit_rows = exact_tokens * rms_rows
    normed = (unit_rows * norm_gain).astype(BF)
    load = jnp.concatenate(
        [
            dot(pick_rows, normed).astype(BF),
            jnp.broadcast_to(slot_block.astype(BF), (slot_total, LANES)),
        ],
        axis=1,
    )
    arrived = exchange(load, owner_count)

    cot_load = (slot_weight * dot(pick_rows, out_cotangent)).astype(BF)
    cot_load, arrived = lax.optimization_barrier((cot_load, arrived))
    cot_rows = exchange(cot_load, owner_count)

    normed_rows = arrived[:, :features]
    block_here = arrived[:, features : features + 1].astype(jnp.int32) - 1
    row_block = jnp.arange(value_rows, dtype=jnp.int32) // BLOCK
    in_block = block_here == row_block[None, :]

    query_rows = dot(normed_rows, weight_full).astype(BF)
    scores = dot(query_rows, values, 1, 1) * score_scale
    sigmoid_of = jax.nn.sigmoid(scores)
    gate_values = jnp.where(in_block, sigmoid_of, 0.0).astype(BF)
    parts_back = exchange(dot(gate_values, values).astype(BF), owner_count)
    cot_scores = dot(cot_rows, values, 1, 1)
    score_grads = jnp.where(
        in_block, cot_scores * sigmoid_of * (1.0 - sigmoid_of) * score_scale, 0.0
    ).astype(BF)
    grads_back = exchange(dot(score_grads, values).astype(BF), owner_count)
    grad_values = (dot(gate_values, cot_rows, 0, 0) + dot(score_grads, query_rows, 0, 0)).astype(BF)

    mixed = sum(
        weights[:, k][:, None] * dot(p.astype(BF), parts_back, 0, 0) for k, p in enumerate(picks)
    )
    layer_out = exact_tokens + mixed
    query_grad = dot(pick_rows, grads_back, 0, 0).astype(BF)
    unit_grad = dot(query_grad, weight_full, 1, 1) * norm_gain
    grad_tokens = out_cotangent.astype(F32) + rms_rows * (
        unit_grad - unit_rows * jnp.mean(unit_grad * unit_rows, axis=1, keepdims=True)
    )
    return (layer_out, grad_tokens, grad_values)


def solution(mesh):
    rows = P(AXES, None)
    return jax.shard_map(
        body,
        mesh=mesh,
        in_specs=(rows, P(), P(None, "dp"), rows, rows, rows, rows),
        out_specs=(rows, rows, rows),
        check_vma=False,
    )
```

```python
import jax
import jax.numpy as jnp
from jax import lax
from jax.sharding import Mesh, PartitionSpec as P

BLOCK = 64
LANES = 128
AXES = ("dp", "half", "near")
NEAR = ("dp", "near")
BF = jnp.bfloat16
F32 = jnp.float32


def dot(left, right, left_dim=1, right_dim=0):
    return lax.dot_general(
        left, right, (((left_dim,), (right_dim,)), ((), ())), preferred_element_type=F32
    )


def exchange(rows, owner_count):
    slots, features = rows.shape
    out = lax.all_to_all(
        rows.reshape(owner_count, slots // owner_count, features),
        NEAR,
        split_axis=0,
        concat_axis=0,
        tiled=True,
    )
    return out.reshape(slots, features)


def across(rows):
    return lax.ppermute(rows, "half", [(0, 1), (1, 0)])


def slots_of(block_ids, lookup_weights, near_count, capacity, span_blocks):
    token_count, top_count = block_ids.shape
    pair_count = token_count * top_count
    owner_of = block_ids // span_blocks
    half_of = owner_of // lax.axis_size("near") % 2
    here = half_of == lax.axis_index("half")
    near_of = owner_of // (2 * lax.axis_size("near")) * lax.axis_size("near")
    near_of = near_of + owner_of % lax.axis_size("near")
    near_of = jnp.where(here, near_of, near_count).reshape(pair_count)
    earlier = (
        jnp.arange(pair_count)[:, None] > jnp.arange(pair_count)[None, :]
    ).astype(BF)
    hits = near_of[:, None] == jnp.arange(near_count, dtype=jnp.int32)[None, :]
    ranks = dot(earlier, hits.astype(BF))
    slot_of = jnp.sum(jnp.where(hits, ranks, 0.0), axis=1).astype(jnp.int32)
    target = (near_of * capacity + slot_of).reshape(token_count, top_count)
    slot_ids = jnp.arange(near_count * capacity, dtype=jnp.int32)
    picks = [(target[:, k][None, :] == slot_ids[:, None]) for k in range(top_count)]
    pick_rows = sum(p.astype(BF) for p in picks)
    slot_weight = sum(
        jnp.sum(jnp.where(p, lookup_weights[:, k][None, :], 0.0), axis=1, keepdims=True)
        for k, p in enumerate(picks)
    )
    local_next = block_ids % span_blocks + 1
    slot_block = sum(
        jnp.sum(jnp.where(p, local_next[:, k][None, :], 0), axis=1, keepdims=True)
        for k, p in enumerate(picks)
    )
    return picks, pick_rows, slot_weight, slot_block


def body(tokens, norm_gain, query_weight, values, blocks, weights, out_cotangent):
    token_count, features = tokens.shape
    top_count = blocks.shape[1]
    value_rows = values.shape[0]
    span_blocks = value_rows // BLOCK
    near_count = lax.axis_size("dp") * lax.axis_size("near")
    capacity = token_count * top_count // near_count
    score_scale = float(features) ** (-0.5)
    weight_full = lax.all_gather(query_weight, "dp", axis=1, tiled=True)

    exact_tokens = tokens.astype(F32)
    rms_rows = lax.rsqrt(jnp.mean(exact_tokens * exact_tokens, axis=1, keepdims=True) + 1e-06)
    unit_rows = exact_tokens * rms_rows
    normed = (unit_rows * norm_gain).astype(BF)

    facts = across(jnp.concatenate([blocks.astype(F32), weights], axis=1))
    far_blocks = facts[:, :top_count].astype(jnp.int32)
    far_weights = facts[:, top_count:]
    far_normed = across(normed)
    far_cot = across(out_cotangent)

    row_block = jnp.arange(value_rows, dtype=jnp.int32) // BLOCK

    def send(block_ids, lookup_weights, normed_part, cot_part):
        picks, pick_rows, slot_weight, slot_block = slots_of(
            block_ids, lookup_weights, near_count, capacity, span_blocks
        )
        load = jnp.concatenate(
            [
                dot(pick_rows, normed_part).astype(BF),
                (slot_weight * dot(pick_rows, cot_part)).astype(BF),
                jnp.broadcast_to(slot_block.astype(BF), (slot_block.shape[0], LANES)),
            ],
            axis=1,
        )
        return picks, pick_rows, exchange(load, near_count)

    def look_up(arrived):
        normed_rows = arrived[:, :features]
        cot_rows = arrived[:, features : 2 * features]
        block_here = arrived[:, 2 * features : 2 * features + 1].astype(jnp.int32) - 1
        in_block = block_here == row_block[None, :]
        query_rows = dot(normed_rows, weight_full).astype(BF)
        sigmoid_of = jax.nn.sigmoid(dot(query_rows, values, 1, 1) * score_scale)
        gate_values = jnp.where(in_block, sigmoid_of, 0.0).astype(BF)
        cot_scores = dot(cot_rows, values, 1, 1)
        score_grads = jnp.where(
            in_block, cot_scores * sigmoid_of * (1.0 - sigmoid_of) * score_scale, 0.0
        ).astype(BF)
        back = jnp.concatenate(
            [dot(gate_values, values).astype(BF), dot(score_grads, values).astype(BF)], axis=1
        )
        grads = dot(gate_values, cot_rows, 0, 0) + dot(score_grads, query_rows, 0, 0)
        return back, grads

    def take(returned, lookup_weights, picks, pick_rows):
        mixed = sum(
            lookup_weights[:, k][:, None] * dot(p.astype(BF), returned[:, :features], 0, 0)
            for k, p in enumerate(picks)
        )
        return mixed, dot(pick_rows, returned[:, features:], 0, 0)

    picks, pick_rows, arrived = send(blocks, weights, normed, out_cotangent)
    far_picks, far_pick_rows, far_arrived = send(far_blocks, far_weights, far_normed, far_cot)
    back, grads = look_up(arrived)
    far_back, far_grads = look_up(far_arrived)
    far_mixed, far_query = take(
        exchange(far_back, near_count), far_weights, far_picks, far_pick_rows
    )
    mixed, query_sum = take(exchange(back, near_count), weights, picks, pick_rows)
    other_query = across(far_query.astype(BF))
    other_mixed = across(far_mixed.astype(BF))
    grad_values = (grads + far_grads).astype(BF)

    layer_out = exact_tokens + (mixed + other_mixed.astype(F32))
    query_grad = (query_sum + other_query.astype(F32)).astype(BF)
    unit_grad = dot(query_grad, weight_full, 1, 1) * norm_gain
    grad_tokens = out_cotangent.astype(F32) + rms_rows * (
        unit_grad - unit_rows * jnp.mean(unit_grad * unit_rows, axis=1, keepdims=True)
    )
    return (layer_out, grad_tokens, grad_values)


def solution(mesh):
    rows = P(AXES, None)
    dp_size, mem_size = mesh.devices.shape
    halves = Mesh(mesh.devices.reshape(dp_size, 2, mem_size // 2), AXES)
    return jax.shard_map(
        body,
        mesh=halves,
        in_specs=(rows, P(), P(None, "dp"), rows, rows, rows, rows),
        out_specs=(rows, rows, rows),
        check_vma=False,
    )
```

```python
import jax
import jax.numpy as jnp
from jax import lax
from jax.sharding import Mesh, PartitionSpec as P

BLOCK = 64
LANES = 128
AXES = ("dp", "half", "near")
NEAR = ("dp", "near")
BF = jnp.bfloat16
F32 = jnp.float32


def dot(left, right, left_dim=1, right_dim=0):
    return lax.dot_general(
        left, right, (((left_dim,), (right_dim,)), ((), ())), preferred_element_type=F32
    )


def exchange(rows, owner_count):
    slots, features = rows.shape
    out = lax.all_to_all(
        rows.reshape(owner_count, slots // owner_count, features),
        NEAR,
        split_axis=0,
        concat_axis=0,
        tiled=True,
    )
    return out.reshape(slots, features)


def across(rows):
    return lax.ppermute(rows, "half", [(0, 1), (1, 0)])


def slots_of(block_ids, lookup_weights, near_count, capacity, span_blocks):
    token_count, top_count = block_ids.shape
    pair_count = token_count * top_count
    owner_of = block_ids // span_blocks
    half_of = owner_of // lax.axis_size("near") % 2
    here = half_of == lax.axis_index("half")
    near_of = owner_of // (2 * lax.axis_size("near")) * lax.axis_size("near")
    near_of = near_of + owner_of % lax.axis_size("near")
    near_of = jnp.where(here, near_of, near_count).reshape(pair_count)
    earlier = (
        jnp.arange(pair_count)[:, None] > jnp.arange(pair_count)[None, :]
    ).astype(BF)
    hits = near_of[:, None] == jnp.arange(near_count, dtype=jnp.int32)[None, :]
    ranks = dot(earlier, hits.astype(BF))
    slot_of = jnp.sum(jnp.where(hits, ranks, 0.0), axis=1).astype(jnp.int32)
    target = (near_of * capacity + slot_of).reshape(token_count, top_count)
    slot_ids = jnp.arange(near_count * capacity, dtype=jnp.int32)
    picks = [(target[:, k][None, :] == slot_ids[:, None]) for k in range(top_count)]
    pick_rows = sum(p.astype(BF) for p in picks)
    slot_weight = sum(
        jnp.sum(jnp.where(p, lookup_weights[:, k][None, :], 0.0), axis=1, keepdims=True)
        for k, p in enumerate(picks)
    )
    local_next = block_ids % span_blocks + 1
    slot_block = sum(
        jnp.sum(jnp.where(p, local_next[:, k][None, :], 0), axis=1, keepdims=True)
        for k, p in enumerate(picks)
    )
    return picks, pick_rows, slot_weight, slot_block


def body(tokens, norm_gain, query_weight, values, blocks, weights, out_cotangent):
    token_count, features = tokens.shape
    top_count = blocks.shape[1]
    value_rows = values.shape[0]
    span_blocks = value_rows // BLOCK
    near_count = lax.axis_size("dp") * lax.axis_size("near")
    capacity = token_count * top_count // near_count
    score_scale = float(features) ** (-0.5)
    weight_full = lax.all_gather(query_weight, "dp", axis=1, tiled=True)

    exact_tokens = tokens.astype(F32)
    rms_rows = lax.rsqrt(jnp.mean(exact_tokens * exact_tokens, axis=1, keepdims=True) + 1e-06)
    unit_rows = exact_tokens * rms_rows
    normed = (unit_rows * norm_gain).astype(BF)

    facts = across(jnp.concatenate([blocks.astype(F32), weights], axis=1))
    far_blocks = facts[:, :top_count].astype(jnp.int32)
    far_weights = facts[:, top_count:]
    far_normed = across(normed)
    far_cot = across(out_cotangent)

    row_block = jnp.arange(value_rows, dtype=jnp.int32) // BLOCK

    def send(block_ids, lookup_weights, normed_part, cot_part):
        picks, pick_rows, slot_weight, slot_block = slots_of(
            block_ids, lookup_weights, near_count, capacity, span_blocks
        )
        load = jnp.concatenate(
            [
                dot(pick_rows, normed_part).astype(BF),
                (slot_weight * dot(pick_rows, cot_part)).astype(BF),
                jnp.broadcast_to(slot_block.astype(BF), (slot_block.shape[0], LANES)),
            ],
            axis=1,
        )
        return picks, pick_rows, exchange(load, near_count)

    def look_up(arrived):
        normed_rows = arrived[:, :features]
        cot_rows = arrived[:, features : 2 * features]
        block_here = arrived[:, 2 * features : 2 * features + 1].astype(jnp.int32) - 1
        in_block = block_here == row_block[None, :]
        query_rows = dot(normed_rows, weight_full).astype(BF)
        sigmoid_of = jax.nn.sigmoid(dot(query_rows, values, 1, 1) * score_scale)
        gate_values = jnp.where(in_block, sigmoid_of, 0.0).astype(BF)
        cot_scores = dot(cot_rows, values, 1, 1)
        score_grads = jnp.where(
            in_block, cot_scores * sigmoid_of * (1.0 - sigmoid_of) * score_scale, 0.0
        ).astype(BF)
        back = jnp.concatenate(
            [dot(gate_values, values).astype(BF), dot(score_grads, values).astype(BF)], axis=1
        )
        grads = dot(gate_values, cot_rows, 0, 0) + dot(score_grads, query_rows, 0, 0)
        return back, grads

    def take(returned, lookup_weights, picks, pick_rows):
        mixed = sum(
            lookup_weights[:, k][:, None] * dot(p.astype(BF), returned[:, :features], 0, 0)
            for k, p in enumerate(picks)
        )
        return mixed, dot(pick_rows, returned[:, features:], 0, 0)

    picks, pick_rows, arrived = send(blocks, weights, normed, out_cotangent)
    far_normed, far_cot, arrived = lax.optimization_barrier((far_normed, far_cot, arrived))
    far_picks, far_pick_rows, far_arrived = send(far_blocks, far_weights, far_normed, far_cot)
    back, grads = look_up(arrived)
    far_back, far_grads = look_up(far_arrived)
    far_mixed, far_query = take(
        exchange(far_back, near_count), far_weights, far_picks, far_pick_rows
    )
    far_query, far_mixed, back = lax.optimization_barrier(
        (far_query.astype(BF), far_mixed.astype(BF), back)
    )
    other_query, other_mixed, returned = lax.optimization_barrier(
        (across(far_query), across(far_mixed), exchange(back, near_count))
    )
    mixed, query_sum = take(returned, weights, picks, pick_rows)
    grad_values = (grads + far_grads).astype(BF)

    layer_out = exact_tokens + (mixed + other_mixed.astype(F32))
    query_grad = (query_sum + other_query.astype(F32)).astype(BF)
    unit_grad = dot(query_grad, weight_full, 1, 1) * norm_gain
    grad_tokens = out_cotangent.astype(F32) + rms_rows * (
        unit_grad - unit_rows * jnp.mean(unit_grad * unit_rows, axis=1, keepdims=True)
    )
    return (layer_out, grad_tokens, grad_values)


def solution(mesh):
    rows = P(AXES, None)
    dp_size, mem_size = mesh.devices.shape
    halves = Mesh(mesh.devices.reshape(dp_size, 2, mem_size // 2), AXES)
    return jax.shard_map(
        body,
        mesh=halves,
        in_specs=(rows, P(), P(None, "dp"), rows, rows, rows, rows),
        out_specs=(rows, rows, rows),
        check_vma=False,
    )
```

```python
import jax
import jax.numpy as jnp
from jax import lax
from jax.sharding import PartitionSpec as P

BLOCK = 64
LANES = 128
AXES = ("dp", "mem")
BF = jnp.bfloat16
F32 = jnp.float32


def dot(left, right, left_dim=1, right_dim=0):
    return lax.dot_general(
        left, right, (((left_dim,), (right_dim,)), ((), ())), preferred_element_type=F32
    )


def exchange(rows, owner_count):
    slots, features = rows.shape
    out = lax.all_to_all(
        rows.reshape(owner_count, slots // owner_count, features),
        AXES,
        split_axis=0,
        concat_axis=0,
        tiled=True,
    )
    return out.reshape(slots, features)


def body(tokens, norm_gain, query_weight, values, blocks, weights, out_cotangent):
    token_count, features = tokens.shape
    top_count = blocks.shape[1]
    value_rows = values.shape[0]
    span_blocks = value_rows // BLOCK
    owner_count = lax.axis_size("dp") * lax.axis_size("mem")
    pair_count = token_count * top_count
    capacity = 2 * pair_count // owner_count
    slot_total = owner_count * capacity
    score_scale = float(features) ** (-0.5)
    weight_full = lax.all_gather(query_weight, "dp", axis=1, tiled=True)

    earlier = (
        jnp.arange(pair_count)[:, None] > jnp.arange(pair_count)[None, :]
    ).astype(BF)

    flat_ids = blocks.reshape(pair_count)
    owner_of = flat_ids // span_blocks
    hits = owner_of[:, None] == jnp.arange(owner_count, dtype=jnp.int32)[None, :]
    ranks = dot(earlier, hits.astype(BF))
    slot_of = jnp.sum(jnp.where(hits, ranks, 0.0), axis=1).astype(jnp.int32)
    target = (owner_of * capacity + slot_of).reshape(token_count, top_count)
    slot_ids = jnp.arange(slot_total, dtype=jnp.int32)
    picks = [(target[:, k][None, :] == slot_ids[:, None]) for k in range(top_count)]
    pick_rows = sum(p.astype(BF) for p in picks)
    slot_weight = sum(
        jnp.sum(jnp.where(p, weights[:, k][None, :], 0.0), axis=1, keepdims=True)
        for k, p in enumerate(picks)
    )

    local_next = blocks % span_blocks + 1
    slot_block = sum(
        jnp.sum(jnp.where(p, local_next[:, k][None, :], 0), axis=1, keepdims=True)
        for k, p in enumerate(picks)
    )

    exact_tokens = tokens.astype(F32)
    rms_rows = lax.rsqrt(jnp.mean(exact_tokens * exact_tokens, axis=1, keepdims=True) + 1e-06)
    unit_rows = exact_tokens * rms_rows
    normed = (unit_rows * norm_gain).astype(BF)
    load = jnp.concatenate(
        [
            dot(pick_rows, normed).astype(BF),
            jnp.broadcast_to(slot_block.astype(BF), (slot_total, LANES)),
        ],
        axis=1,
    )
    arrived = exchange(load, owner_count)

    cot_load = (slot_weight * dot(pick_rows, out_cotangent)).astype(BF)
    cot_load, arrived = lax.optimization_barrier((cot_load, arrived))
    cot_rows = exchange(cot_load, owner_count)

    normed_rows = arrived[:, :features]
    block_here = arrived[:, features : features + 1].astype(jnp.int32) - 1
    row_block = jnp.arange(value_rows, dtype=jnp.int32) // BLOCK
    in_block = block_here == row_block[None, :]

    query_rows = dot(normed_rows, weight_full).astype(BF)
    scores = dot(query_rows, values, 1, 1) * score_scale
    sigmoid_of = jax.nn.sigmoid(scores)
    gate_values = jnp.where(in_block, sigmoid_of, 0.0).astype(BF)
    cot_scores = dot(cot_rows, values, 1, 1)
    score_grads = jnp.where(
        in_block, cot_scores * sigmoid_of * (1.0 - sigmoid_of) * score_scale, 0.0
    ).astype(BF)
    back = exchange(
        jnp.concatenate(
            [dot(gate_values, values).astype(BF), dot(score_grads, values).astype(BF)], axis=1
        ),
        owner_count,
    )
    parts_back, grads_back = back[:, :features], back[:, features:]
    grad_values = (dot(gate_values, cot_rows, 0, 0) + dot(score_grads, query_rows, 0, 0)).astype(BF)

    mixed = sum(
        weights[:, k][:, None] * dot(p.astype(BF), parts_back, 0, 0) for k, p in enumerate(picks)
    )
    layer_out = exact_tokens + mixed
    query_grad = dot(pick_rows, grads_back, 0, 0).astype(BF)
    unit_grad = dot(query_grad, weight_full, 1, 1) * norm_gain
    grad_tokens = out_cotangent.astype(F32) + rms_rows * (
        unit_grad - unit_rows * jnp.mean(unit_grad * unit_rows, axis=1, keepdims=True)
    )
    return (layer_out, grad_tokens, grad_values)


def solution(mesh):
    rows = P(AXES, None)
    return jax.shard_map(
        body,
        mesh=mesh,
        in_specs=(rows, P(), P(None, "dp"), rows, rows, rows, rows),
        out_specs=(rows, rows, rows),
        check_vma=False,
    )
```
